256 devices in a mesh: dp: 2 (over x_lo), mp: 128 (over z, x_hi, y, core).
Axes of the slice: x: 4 (x_hi: 2, x_lo: 2; x = x_hi * 2 + x_lo), y: 4, z: 8, core: 2. Of those that a mesh axis runs over, the one named last changes fastest.
Arguments:
- tokens: bfloat16 [512, 4608], P('dp', 'mp'), may hold values from -6 to 6
- teacher: bfloat16 [512, 4608], P('dp', 'mp'), may hold values from -4 to 4
- gate_weight: bfloat16 [4608, 36864], P(None, 'mp'), may hold values from -0.09375 to 0.09375
- up_weight: bfloat16 [4608, 36864], P(None, 'mp'), may hold values from -0.09375 to 0.09375
- down_weight: bfloat16 [36864, 4608], P('mp'), may hold values from -0.125 to 0.125
Outputs:
- student: bfloat16 [512, 4608], P('dp', 'mp')
- grad_gate: bfloat16 [4608, 36864], P('dp', 'mp')
- grad_up: bfloat16 [4608, 36864], P('dp', 'mp')
- grad_down: bfloat16 [36864, 4608], P('mp', 'dp')
The draws below stay inside these ranges and needn't reach their ends.
All inputs are finite; a program needn't handle non-finite values.
Results may differ from the reference program's by a relative error of at most 0.0085.
Values may be sent and summed in bfloat16 or wider, within the bound.
No kernel may reach another device: no remote copies, remote signals or barrier semaphores. Data moves between devices by JAX's collectives and lax.ppermute only.
A program may use at most 128 MiB of HBM per device.

```python
import math
import jax
import jax.numpy as jnp
from jax import lax

D = 4608
FF = 36864
TOKENS = 512


def strengthened(result, rng, source, target, parts, factor):
    owner, partner = [(jnp.arange(result.shape[dim]) // (result.shape[dim] // parts)).reshape([-1 if axis == dim else 1 for axis in range(result.ndim)]) for dim in (source, target)]
    chosen = jax.random.permutation(rng, parts)[partner]
    strong = (owner == chosen) | (owner == (partner + parts // 2) % parts)
    return jnp.where(strong, factor * result, result)


def block_levels(stream_key, shape, split, least, largest):
    gain = 1.0
    for dim, parts in split:
        draws = jax.random.uniform(jax.random.fold_in(jax.random.fold_in(stream_key, 6), dim), (parts,), jnp.float32, least / len(split), largest / len(split))
        gain = gain * jnp.repeat(jnp.exp(draws), shape[dim] // parts).reshape((-1,) + (1,) * (len(shape) - 1 - dim))
    return gain


def gaussian(stream_key, extent, deviation, limit, split=(), kind=jnp.bfloat16):
    drawn = deviation * jax.random.normal(stream_key, extent, jnp.float32)
    if split:
        drawn = drawn * block_levels(stream_key, extent, split, -0.22, 0.18)
    return jnp.clip(drawn, -limit, limit).astype(kind)


def noise_with(rng, extent, spread, bound, cuts, heavy, dtype=jnp.bfloat16):
    result = spread * jax.random.normal(rng, extent, jnp.float32)
    if cuts:
        result = result * block_levels(rng, extent, cuts, -0.22, 0.18)
    return jnp.clip(strengthened(result, jax.random.fold_in(rng, 3), *heavy), -bound, bound).astype(dtype)


def setup_inputs(seed: int = 0) -> dict:
    key_of = jax.random.split(jax.random.key(seed), 6)
    return {
        "tokens": gaussian(key_of[0], (TOKENS, D), 1.0, 6.0, ((0, 2), (1, 128))),
        "teacher": gaussian(key_of[1], (TOKENS, D), 0.6, 4.0, ((0, 2), (1, 128))),
        "gate_weight": gaussian(key_of[2], (D, FF), D ** -0.5, 0.09375, ((1, 128),)),
        "up_weight": gaussian(key_of[3], (D, FF), D ** -0.5, 0.09375, ((1, 128),)),
        "down_weight": noise_with(key_of[4], (FF, D), FF ** -0.5, 0.125, ((0, 128),), (0, 1, 128, 5.5)),
    }


def reference(tokens, teacher, gate_weight, up_weight, down_weight):
    gate = jnp.dot(tokens, gate_weight, preferred_element_type=jnp.float32)
    upper = jnp.dot(tokens, up_weight, preferred_element_type=jnp.float32)
    sigma = jax.nn.sigmoid(gate)
    hidden = (gate * sigma * upper).astype(jnp.bfloat16)
    summed = jnp.dot(hidden, down_weight, preferred_element_type=jnp.float32)
    student = summed.astype(jnp.bfloat16)
    factor = 1.0 / math.sqrt(TOKENS)
    errors = ((summed - teacher.astype(jnp.float32)) * factor).astype(jnp.bfloat16)
    back = lax.dot_general(errors, down_weight, (((1,), (1,)), ((), ())), preferred_element_type=jnp.float32)
    up_back = (back * gate * sigma).astype(jnp.bfloat16)
    gate_back = (back * upper * sigma * (1.0 + gate * (1.0 - sigma))).astype(jnp.bfloat16)
    contract = (((0,), (0,)), ((), ()))
    grad_gate = lax.dot_general(tokens, gate_back, contract, preferred_element_type=jnp.float32)
    grad_up = lax.dot_general(tokens, up_back, contract, preferred_element_type=jnp.float32)
    grad_down = lax.dot_general(hidden, errors, contract, preferred_element_type=jnp.float32)
    return (student, grad_gate.astype(jnp.bfloat16), grad_up.astype(jnp.bfloat16), grad_down.astype(jnp.bfloat16))
```

```python
import math

import jax
import jax.numpy as jnp
from jax import lax
from jax.sharding import Mesh, PartitionSpec as P

BF = jnp.bfloat16
F32 = jnp.float32
ZX = ("z", "xh")


def swap(x, axis):
    return lax.ppermute(x, axis, [(0, 1), (1, 0)])


def shift(x, axis, k):
    n = lax.axis_size(axis)
    return lax.ppermute(x, axis, [(i, (i + k) % n) for i in range(n)])


def pair_block(x, c):
    xt = x.T
    half = xt.shape[1] // 2
    first, second = xt[:, :half], xt[:, half:]
    mine = jnp.where(c == 0, first, second)
    theirs = swap(jnp.where(c == 0, second, first), "c")
    low = jnp.where(c == 0, mine, theirs)
    high = jnp.where(c == 0, theirs, mine)
    return jnp.concatenate([low, high], axis=0)


def unpair_block(block, c):
    rows = block.shape[0] // 2
    low, high = block[:rows], block[rows:]
    mine = jnp.where(c == 0, low, high)
    theirs = swap(jnp.where(c == 0, high, low), "c")
    first = jnp.where(c == 0, mine, theirs)
    second = jnp.where(c == 0, theirs, mine)
    return jnp.concatenate([first, second], axis=1).T


def gather_half(block, y):
    groups = lax.axis_size("z") * lax.axis_size("xh")
    ny = lax.axis_size("y")
    copies = jnp.broadcast_to(block[None], (groups,) + block.shape)
    part = lax.all_to_all(copies, ZX, 0, 0)
    whole = jnp.zeros((groups, ny) + block.shape, block.dtype)
    whole = lax.dynamic_update_slice_in_dim(whole, part[:, None], y, 1)
    for k in range(1, ny):
        piece = shift(part, "y", k)
        whole = lax.dynamic_update_slice_in_dim(whole, piece[:, None], lax.rem(y - k + ny, ny), 1)
    return whole


def scatter_half(terms, y):
    ny = lax.axis_size("y")
    narrow = terms.astype(BF)
    total = lax.dynamic_index_in_dim(terms, y, 1, keepdims=False)
    for k in range(1, ny):
        sent = lax.dynamic_index_in_dim(narrow, lax.rem(y + k, ny), 1, keepdims=False)
        total = total + shift(sent, "y", k).astype(F32)
    pieces = lax.all_to_all(total.astype(BF), ZX, 0, 0)
    return jnp.sum(pieces.astype(F32), axis=0)


def shards(tokens, teacher, gate_weight, up_weight, down_weight):
    c, y, d = lax.axis_index("c"), lax.axis_index("y"), lax.axis_index("dp")
    features = gate_weight.shape[0]
    half = features // 2
    factor = 1.0 / math.sqrt(tokens.shape[0] * lax.axis_size("dp"))

    x_mine = gather_half(pair_block(tokens, c), y)
    teach = pair_block(teacher, c).astype(F32)
    shape4 = x_mine.shape
    x_mine = x_mine.reshape(features, -1)
    x_other = swap(x_mine, "c")
    x = jnp.concatenate([x_mine, x_other], axis=1)

    first = (((0,), (0,)), ((), ()))
    gate = lax.dot_general(x, gate_weight, first, preferred_element_type=F32)
    upper = lax.dot_general(x, up_weight, first, preferred_element_type=F32)
    sigma = jax.nn.sigmoid(gate)
    hidden = (gate * sigma * upper).astype(BF)

    terms = lax.dot_general(down_weight, hidden, (((0,), (1,)), ((), ())), preferred_element_type=F32)
    count = shape4[-1]
    received = swap(terms[:, count:].astype(BF), "c")
    pair = (terms[:, :count] + received.astype(F32)).reshape(shape4)
    summed = scatter_half(pair, y)
    student = unpair_block(summed.astype(BF), c)
    errors = ((summed - teach) * factor).astype(BF)

    e_mine = gather_half(errors, y).reshape(features, -1)
    e_other = swap(e_mine, "c")
    e = jnp.concatenate([e_mine, e_other], axis=1)
    back = lax.dot_general(e, down_weight, (((0,), (1,)), ((), ())), preferred_element_type=F32)
    up_back = (back * gate * sigma).astype(BF)
    gate_back = (back * upper * sigma * (1.0 + gate * (1.0 - sigma))).astype(BF)

    def other_half(z):
        return lax.dynamic_slice_in_dim(z, (1 - d) * half, half, 0)

    def own_half(z):
        return lax.dynamic_slice_in_dim(z, d * half, half, 0)

    xp_mine = swap(other_half(x_mine), "dp")
    xp = jnp.concatenate([xp_mine, swap(xp_mine, "c")], axis=1)
    ep_mine = swap(other_half(e_mine), "dp")
    ep = jnp.concatenate([ep_mine, swap(ep_mine, "c")], axis=1)
    xo, eo = own_half(x), own_half(e)
    hidden_p = swap(hidden, "dp")
    up_back_p = swap(up_back, "dp")
    gate_back_p = swap(gate_back, "dp")

    def dot(a, b, dims):
        return lax.dot_general(a, b, (dims, ((), ())), preferred_element_type=F32)

    grad_gate = dot(xo, gate_back, ((1,), (0,))) + dot(xp, gate_back_p, ((1,), (0,)))
    grad_up = dot(xo, up_back, ((1,), (0,))) + dot(xp, up_back_p, ((1,), (0,)))
    grad_down = dot(hidden, eo, ((0,), (1,))) + dot(hidden_p, ep, ((0,), (1,)))
    return student, grad_gate.astype(BF), grad_up.astype(BF), grad_down.astype(BF)


def solution(mesh):
    mp = ("z", "xh", "y", "c")
    fine = Mesh(mesh.devices.reshape(2, 8, 2, 4, 2), ("dp",) + mp)
    return jax.shard_map(
        shards,
        mesh=fine,
        in_specs=(P("dp", mp), P("dp", mp), P(None, mp), P(None, mp), P(mp, None)),
        out_specs=(P("dp", mp), P("dp", mp), P("dp", mp), P(mp, "dp")),
        check_vma=False,
    )
```

```python
import functools
import math

import jax
import jax.numpy as jnp
from jax import lax
from jax.experimental import pallas as pl
from jax.experimental.pallas import tpu as pltpu
from jax.experimental.layout import Layout, with_layout_constraint
from jax.sharding import Mesh, PartitionSpec as P

BF = jnp.bfloat16
F32 = jnp.float32
ZX = ("z", "xh")


def swap(x, axis):
    return lax.ppermute(x, axis, [(0, 1), (1, 0)])


def shift(x, axis, k):
    n = lax.axis_size(axis)
    return lax.ppermute(x, axis, [(i, (i + k) % n) for i in range(n)])


def pair_block(x, c):
    xt = x.T
    half = xt.shape[1] // 2
    first, second = xt[:, :half], xt[:, half:]
    mine = jnp.where(c == 0, first, second)
    theirs = swap(jnp.where(c == 0, second, first), "c")
    low = jnp.where(c == 0, mine, theirs)
    high = jnp.where(c == 0, theirs, mine)
    return jnp.concatenate([low, high], axis=0)


def unpair_block(block, c):
    rows = block.shape[0] // 2
    low, high = block[:rows], block[rows:]
    mine = jnp.where(c == 0, low, high)
    theirs = swap(jnp.where(c == 0, high, low), "c")
    first = jnp.where(c == 0, mine, theirs)
    second = jnp.where(c == 0, theirs, mine)
    return jnp.concatenate([first, second], axis=1).T


def gather_zx(block):
    groups = lax.axis_size("z") * lax.axis_size("xh")
    copies = jnp.broadcast_to(block[None], (groups,) + block.shape)
    return lax.all_to_all(copies, ZX, 0, 0)


def gather_y(part, y, axis, *meanwhile):
    ny = lax.axis_size("y")
    part = jnp.expand_dims(part, axis)
    pieces = {k: shift(part, "y", k) for k in (2, 1, 3)}
    whole = jnp.broadcast_to(part, part.shape[:axis] + (ny,) + part.shape[axis + 1 :])
    pieces[1], whole, *meanwhile = barrier(pieces[1], whole, *meanwhile)
    for k in (1, 3, 2):
        whole = lax.dynamic_update_slice_in_dim(whole, pieces[k], lax.rem(y - k + ny, ny), axis)
    return (whole, *meanwhile)


def dot(a, b, i, j):
    return lax.dot_general(a, b, (((i,), (j,)), ((), ())), preferred_element_type=F32)


def row_major(x):
    return with_layout_constraint(x, Layout(major_to_minor=tuple(range(x.ndim))))


def barrier(*values):
    return lax.optimization_barrier(values)


def regroup_kernel(rows, y_ref, w_ref, out_ref):
    ny = out_ref.shape[0]
    groups = out_ref.shape[2] // rows
    for p in range(ny):
        k = lax.rem(p + ny - y_ref[0], ny)
        for g in range(groups):
            start = (g * ny + p) * rows
            out_ref[k, :, g * rows : (g + 1) * rows] = w_ref[:, start : start + rows]


def regroup(weight, y, ny, rows):
    units, features = weight.shape
    block = 32
    return pl.pallas_call(
        functools.partial(regroup_kernel, rows),
        grid_spec=pltpu.PrefetchScalarGridSpec(
            num_scalar_prefetch=1,
            grid=(units // block,),
            in_specs=[pl.BlockSpec((block, features), lambda i, y: (i, 0))],
            out_specs=pl.BlockSpec((ny, block, features // ny), lambda i, y: (0, i, 0)),
        ),
        out_shape=jax.ShapeDtypeStruct((ny, units, features // ny), weight.dtype),
        cost_estimate=pl.CostEstimate(flops=0, bytes_accessed=4 * units * features, transcendentals=0),
        name="regroup",
    )(y.reshape(1), weight)


def shards(tokens, teacher, gate_weight, up_weight, down_weight):
    c, y, d = lax.axis_index("c"), lax.axis_index("y"), lax.axis_index("dp")
    ny = lax.axis_size("y")
    features, units = gate_weight.shape
    groups = lax.axis_size("z") * lax.axis_size("xh")
    rows = features // (groups * ny)
    half = features // 2
    factor = 1.0 / math.sqrt(tokens.shape[0] * lax.axis_size("dp"))

    block, down_weight = barrier(pair_block(tokens, c), down_weight)
    part = gather_zx(block)
    down = regroup(down_weight, y, ny, rows)
    part, down = barrier(part, down)
    (x_mine,) = gather_y(part, y, 1)
    x_mine = x_mine.reshape(features, -1)
    count = x_mine.shape[1]
    x = jnp.concatenate([x_mine, swap(x_mine, "c")], axis=1)

    gate = dot(gate_weight, x, 0, 0)
    upper = dot(up_weight, x, 0, 0)
    sigma = jax.nn.sigmoid(gate)
    silu = gate * sigma
    slope = (upper * sigma * (1.0 + gate * (1.0 - sigma))).astype(BF)
    hidden = (silu * upper).astype(BF)
    silu = silu.astype(BF)

    def pair(k):
        other = swap(row_major(dot(down[k], hidden[:, count:], 0, 0).astype(BF)), "c")
        return row_major(dot(down[k], hidden[:, :count], 0, 0)) + other.astype(F32)

    arrived = [shift(pair(k).astype(BF), "y", k) for k in (2, 1, 3)]
    total = pair(0)
    for piece in arrived:
        total = total + piece.astype(F32)
    held_p = swap(jnp.stack([hidden, silu, slope]), "dp")
    teach = pair_block(teacher, c).astype(F32)
    total, held_p, teach = barrier(total.astype(BF), held_p, teach)
    sums = lax.all_to_all(total.reshape(groups, rows, count), ZX, 0, 0)
    summed = jnp.sum(sums.astype(F32), axis=0)
    student = unpair_block(summed.astype(BF), c)
    errors = ((summed - teach) * factor).astype(BF)

    e_part = gather_zx(errors)
    xs = lax.dynamic_slice_in_dim(x_mine, (1 - d) * half, half, 0)
    e_part, student, xs = barrier(e_part, student, xs)
    keep, give = d * (groups // 2), (1 - d) * (groups // 2)
    e_got = swap(lax.dynamic_slice_in_dim(e_part, give, groups // 2, 0), "dp")
    xp_mine = swap(xs, "dp")
    e_pieces = {0: e_part, **{k: shift(e_part, "y", k) for k in (2, 1, 3)}}
    back = 0.0
    kept = {}
    for k in (0, 1, 3, 2):
        piece = e_pieces[k].reshape(groups * rows, count)
        other = swap(piece, "c")
        if k:
            other, back = barrier(other, back)
        piece = jnp.concatenate([piece, other], axis=1)
        kept[k] = lax.dynamic_slice_in_dim(piece.reshape(groups, rows, 2 * count), keep, groups // 2, 0)
        back = back + dot(down[(ny - k) % ny], piece, 1, 0)
    narrow, e_got = barrier(back.astype(BF), e_got)
    back_p = swap(narrow, "dp").astype(F32)
    got_pieces = {0: e_got, **{k: shift(e_got, "y", k) for k in (2, 1, 3)}}
    hidden_p, silu_p, slope_p = held_p[0], held_p[1].astype(F32), held_p[2].astype(F32)
    up_back = jnp.concatenate([(back * silu).astype(BF), (back_p * silu_p).astype(BF)], axis=1)
    gate_back = jnp.concatenate([(back * slope).astype(BF), (back_p * slope_p).astype(BF)], axis=1)

    def assembled(pieces):
        whole = jnp.broadcast_to(pieces[0][:, None], (groups // 2, ny) + pieces[0].shape[1:])
        for k in (1, 3, 2):
            whole = lax.dynamic_update_slice_in_dim(whole, pieces[k][:, None], lax.rem(y - k + ny, ny), 1)
        return whole.reshape(half, -1)

    eo, ep_mine = assembled(kept), assembled(got_pieces)
    errors_both = jnp.concatenate([eo, ep_mine, swap(ep_mine, "c")], axis=1)
    xo = lax.dynamic_slice_in_dim(x, d * half, half, 0)
    x_both = jnp.concatenate([xo, xp_mine, swap(xp_mine, "c")], axis=1)
    grad_gate = dot(x_both, gate_back, 1, 1)
    grad_up = dot(x_both, up_back, 1, 1)
    grad_down = dot(jnp.concatenate([hidden, hidden_p], axis=1), errors_both, 1, 1)
    return student, grad_gate.astype(BF), grad_up.astype(BF), grad_down.astype(BF)


def solution(mesh):
    mp = ("z", "xh", "y", "c")
    fine = Mesh(mesh.devices.reshape(2, 8, 2, 4, 2), ("dp",) + mp)
    return jax.shard_map(
        shards,
        mesh=fine,
        in_specs=(P("dp", mp), P("dp", mp), P(None, mp), P(None, mp), P(mp, None)),
        out_specs=(P("dp", mp), P("dp", mp), P("dp", mp), P(mp, "dp")),
        check_vma=False,
    )
```

```python
import functools
import math

import jax
import jax.numpy as jnp
from jax import lax
from jax.experimental import pallas as pl
from jax.experimental.pallas import tpu as pltpu
from jax.experimental.layout import Layout, with_layout_constraint
from jax.sharding import Mesh, PartitionSpec as P

BF = jnp.bfloat16
F32 = jnp.float32
ZX = ("z", "xh")


def swap(x, axis):
    return lax.ppermute(x, axis, [(0, 1), (1, 0)])


def shift(x, axis, k):
    n = lax.axis_size(axis)
    return lax.ppermute(x, axis, [(i, (i + k) % n) for i in range(n)])


def pair_block(x, c):
    xt = x.T
    half = xt.shape[1] // 2
    first, second = xt[:, :half], xt[:, half:]
    mine = jnp.where(c == 0, first, second)
    theirs = swap(jnp.where(c == 0, second, first), "c")
    low = jnp.where(c == 0, mine, theirs)
    high = jnp.where(c == 0, theirs, mine)
    return jnp.concatenate([low, high], axis=0)


def unpair_block(block, c):
    rows = block.shape[0] // 2
    low, high = block[:rows], block[rows:]
    mine = jnp.where(c == 0, low, high)
    theirs = swap(jnp.where(c == 0, high, low), "c")
    first = jnp.where(c == 0, mine, theirs)
    second = jnp.where(c == 0, theirs, mine)
    return jnp.concatenate([first, second], axis=1).T


def gather_zx(block):
    groups = lax.axis_size("z") * lax.axis_size("xh")
    copies = jnp.broadcast_to(block[None], (groups,) + block.shape)
    return lax.all_to_all(copies, ZX, 0, 0)


def gather_y(part, y, axis, *meanwhile):
    ny = lax.axis_size("y")
    part = jnp.expand_dims(part, axis)
    pieces = {k: shift(part, "y", k) for k in (2, 1, 3)}
    whole = jnp.broadcast_to(part, part.shape[:axis] + (ny,) + part.shape[axis + 1 :])
    pieces[1], whole, *meanwhile = barrier(pieces[1], whole, *meanwhile)
    for k in (1, 3, 2):
        whole = lax.dynamic_update_slice_in_dim(whole, pieces[k], lax.rem(y - k + ny, ny), axis)
    return (whole, *meanwhile)


def dot(a, b, i, j):
    return lax.dot_general(a, b, (((i,), (j,)), ((), ())), preferred_element_type=F32)


def row_major(x):
    return with_layout_constraint(x, Layout(major_to_minor=tuple(range(x.ndim))))


def barrier(*values):
    return lax.optimization_barrier(values)


def regroup_kernel(rows, y_ref, w_ref, out_ref):
    ny = out_ref.shape[0]
    groups = out_ref.shape[2] // rows
    for p in range(ny):
        k = lax.rem(p + ny - y_ref[0], ny)
        for g in range(groups):
            start = (g * ny + p) * rows
            out_ref[k, :, g * rows : (g + 1) * rows] = w_ref[:, start : start + rows]


def regroup(weight, y, ny, rows):
    units, features = weight.shape
    block = units // 3
    return pl.pallas_call(
        functools.partial(regroup_kernel, rows),
        grid_spec=pltpu.PrefetchScalarGridSpec(
            num_scalar_prefetch=1,
            grid=(units // block,),
            in_specs=[pl.BlockSpec((block, features), lambda i, y: (i, 0))],
            out_specs=pl.BlockSpec((ny, block, features // ny), lambda i, y: (0, i, 0)),
        ),
        out_shape=jax.ShapeDtypeStruct((ny, units, features // ny), weight.dtype),
        cost_estimate=pl.CostEstimate(flops=0, bytes_accessed=4 * units * features, transcendentals=0),
        name="regroup",
    )(y.reshape(1), weight)


def shards(tokens, teacher, gate_weight, up_weight, down_weight):
    c, y, d = lax.axis_index("c"), lax.axis_index("y"), lax.axis_index("dp")
    ny = lax.axis_size("y")
    features, units = gate_weight.shape
    groups = lax.axis_size("z") * lax.axis_size("xh")
    rows = features // (groups * ny)
    half = features // 2
    factor = 1.0 / math.sqrt(tokens.shape[0] * lax.axis_size("dp"))

    block, down_weight = barrier(pair_block(tokens, c), down_weight)
    part = gather_zx(block)
    down = regroup(down_weight, y, ny, rows)
    part, down = barrier(part, down)
    (x_mine,) = gather_y(part, y, 1)
    x_mine = x_mine.reshape(features, -1)
    count = x_mine.shape[1]
    x_other = swap(x_mine, "c")

    def forward(tokens_half):
        gate = dot(gate_weight, tokens_half, 0, 0)
        upper = dot(up_weight, tokens_half, 0, 0)
        sigma = jax.nn.sigmoid(gate)
        silu = gate * sigma
        slope = upper * sigma * (1.0 + gate * (1.0 - sigma))
        return [t.astype(BF) for t in (silu * upper, silu, slope)]

    held_mine, held_other = forward(x_mine), forward(x_other)
    hidden, silu, slope = (jnp.concatenate(t, axis=1) for t in zip(held_mine, held_other))

    def pair(k):
        other = swap(row_major(dot(down[k], held_other[0], 0, 0).astype(BF)), "c")
        return row_major(dot(down[k], held_mine[0], 0, 0)) + other.astype(F32)

    arrived = [shift(pair(k).astype(BF), "y", k) for k in (2, 1, 3)]
    total = pair(0)
    for piece in arrived:
        total = total + piece.astype(F32)
    held_p = swap(jnp.stack([hidden, silu, slope]), "dp")
    teach = pair_block(teacher, c).astype(F32)
    total, held_p, teach = barrier(total.astype(BF), held_p, teach)
    sums = lax.all_to_all(total.reshape(groups, rows, count), ZX, 0, 0)
    summed = jnp.sum(sums.astype(F32), axis=0)
    student = unpair_block(summed.astype(BF), c)
    errors = ((summed - teach) * factor).astype(BF)

    xs = lax.dynamic_slice_in_dim(x_mine, (1 - d) * half, half, 0)
    errors, xs, x_mine, x_other = barrier(errors, xs, x_mine, x_other)
    xp_mine = swap(xs, "dp")
    e_part = gather_zx(errors)
    xo = [lax.dynamic_slice_in_dim(t, d * half, half, 0) for t in (x_mine, x_other)]
    e_part, student, *xo = barrier(e_part, student, *xo)
    keep, give = d * (groups // 2), (1 - d) * (groups // 2)
    e_got = swap(lax.dynamic_slice_in_dim(e_part, give, groups // 2, 0), "dp")
    e_pieces = {0: e_part, **{k: shift(e_part, "y", k) for k in (2, 1, 3)}}
    back = 0.0
    kept = {}
    for k in (0, 1, 3, 2):
        piece = e_pieces[k].reshape(groups * rows, count)
        if k == 1:
            piece, back = barrier(piece, back)
        other = swap(piece, "c")
        if k:
            other, back = barrier(other, back)
        piece = jnp.concatenate([piece, other], axis=1)
        kept[k] = lax.dynamic_slice_in_dim(piece.reshape(groups, rows, 2 * count), keep, groups // 2, 0)
        back = back + dot(down[(ny - k) % ny], piece, 1, 0)
    narrow, e_got = barrier(back.astype(BF), e_got)
    back_p = swap(narrow, "dp").astype(F32)
    got_pieces = {0: e_got, **{k: shift(e_got, "y", k) for k in (2, 1, 3)}}
    hidden_p, silu_p, slope_p = held_p[0], held_p[1].astype(F32), held_p[2].astype(F32)
    up_back = jnp.concatenate([(back * silu).astype(BF), (back_p * silu_p).astype(BF)], axis=1)
    gate_back = jnp.concatenate([(back * slope).astype(BF), (back_p * slope_p).astype(BF)], axis=1)

    def assembled(pieces):
        whole = jnp.broadcast_to(pieces[0][:, None], (groups // 2, ny) + pieces[0].shape[1:])
        for k in (1, 3, 2):
            whole = lax.dynamic_update_slice_in_dim(whole, pieces[k][:, None], lax.rem(y - k + ny, ny), 1)
        return whole.reshape(half, -1)

    x_both = jnp.concatenate([*xo, xp_mine, swap(xp_mine, "c")], axis=1)
    grad_gate = dot(x_both, gate_back, 1, 1)
    grad_up = dot(x_both, up_back, 1, 1)
    grad_gate, *got_late = barrier(grad_gate, *(got_pieces[k] for k in (1, 2, 3)))
    eo, ep_mine = assembled(kept), assembled(dict(enumerate([got_pieces[0], *got_late])))
    errors_both = jnp.concatenate([eo, ep_mine, swap(ep_mine, "c")], axis=1)
    grad_down = dot(jnp.concatenate([hidden, hidden_p], axis=1), errors_both, 1, 1)
    return student, grad_gate.astype(BF), grad_up.astype(BF), grad_down.astype(BF)


def solution(mesh):
    mp = ("z", "xh", "y", "c")
    fine = Mesh(mesh.devices.reshape(2, 8, 2, 4, 2), ("dp",) + mp)
    return jax.shard_map(
        shards,
        mesh=fine,
        in_specs=(P("dp", mp), P("dp", mp), P(None, mp), P(None, mp), P(mp, None)),
        out_specs=(P("dp", mp), P("dp", mp), P("dp", mp), P(mp, "dp")),
        check_vma=False,
    )
```

```python
import functools
import math

import jax
import jax.numpy as jnp
from jax import lax
from jax.experimental import pallas as pl
from jax.experimental.pallas import tpu as pltpu
from jax.experimental.layout import Layout, with_layout_constraint
from jax.sharding import Mesh, PartitionSpec as P

BF = jnp.bfloat16
F32 = jnp.float32
ZX = ("z", "xh")


def swap(x, axis):
    return lax.ppermute(x, axis, [(0, 1), (1, 0)])


def shift(x, axis, k):
    n = lax.axis_size(axis)
    return lax.ppermute(x, axis, [(i, (i + k) % n) for i in range(n)])


def pair_block(x, c):
    xt = x.T
    half = xt.shape[1] // 2
    first, second = xt[:, :half], xt[:, half:]
    mine = jnp.where(c == 0, first, second)
    theirs = swap(jnp.where(c == 0, second, first), "c")
    low = jnp.where(c == 0, mine, theirs)
    high = jnp.where(c == 0, theirs, mine)
    return jnp.concatenate([low, high], axis=0)


def unpair_block(block, c):
    rows = block.shape[0] // 2
    low, high = block[:rows], block[rows:]
    mine = jnp.where(c == 0, low, high)
    theirs = swap(jnp.where(c == 0, high, low), "c")
    first = jnp.where(c == 0, mine, theirs)
    second = jnp.where(c == 0, theirs, mine)
    return jnp.concatenate([first, second], axis=1).T


def gather_zx(block):
    groups = lax.axis_size("z") * lax.axis_size("xh")
    copies = jnp.broadcast_to(block[None], (groups,) + block.shape)
    return lax.all_to_all(copies, ZX, 0, 0)


def gather_y(part, y, axis, *meanwhile):
    ny = lax.axis_size("y")
    part = jnp.expand_dims(part, axis)
    pieces = {k: shift(part, "y", k) for k in (2, 1, 3)}
    whole = jnp.broadcast_to(part, part.shape[:axis] + (ny,) + part.shape[axis + 1 :])
    pieces[1], whole, *meanwhile = barrier(pieces[1], whole, *meanwhile)
    for k in (1, 3, 2):
        whole = lax.dynamic_update_slice_in_dim(whole, pieces[k], lax.rem(y - k + ny, ny), axis)
    return (whole, *meanwhile)


def dot(a, b, i, j):
    return lax.dot_general(a, b, (((i,), (j,)), ((), ())), preferred_element_type=F32)


def row_major(x):
    return with_layout_constraint(x, Layout(major_to_minor=tuple(range(x.ndim))))


def barrier(*values):
    return lax.optimization_barrier(values)


def regroup_kernel(rows, y_ref, w_ref, out_ref):
    ny = out_ref.shape[0]
    groups = out_ref.shape[2] // rows
    for p in range(ny):
        k = lax.rem(p + ny - y_ref[0], ny)
        for g in range(groups):
            start = (g * ny + p) * rows
            out_ref[k, :, g * rows : (g + 1) * rows] = w_ref[:, start : start + rows]


def regroup(weight, y, ny, rows):
    units, features = weight.shape
    block = units // 3
    return pl.pallas_call(
        functools.partial(regroup_kernel, rows),
        grid_spec=pltpu.PrefetchScalarGridSpec(
            num_scalar_prefetch=1,
            grid=(units // block,),
            in_specs=[pl.BlockSpec((block, features), lambda i, y: (i, 0))],
            out_specs=pl.BlockSpec((ny, block, features // ny), lambda i, y: (0, i, 0)),
        ),
        out_shape=jax.ShapeDtypeStruct((ny, units, features // ny), weight.dtype),
        cost_estimate=pl.CostEstimate(flops=0, bytes_accessed=4 * units * features, transcendentals=0),
        name="regroup",
    )(y.reshape(1), weight)


def shards(tokens, teacher, gate_weight, up_weight, down_weight):
    c, y, d = lax.axis_index("c"), lax.axis_index("y"), lax.axis_index("dp")
    ny = lax.axis_size("y")
    features, units = gate_weight.shape
    groups = lax.axis_size("z") * lax.axis_size("xh")
    rows = features // (groups * ny)
    half = features // 2
    factor = 1.0 / math.sqrt(tokens.shape[0] * lax.axis_size("dp"))

    block, down_weight = barrier(pair_block(tokens, c), down_weight)
    part = gather_zx(block)
    down = regroup(down_weight, y, ny, rows)
    part, down = barrier(part, down)
    (x_mine,) = gather_y(part, y, 1)
    x_mine = x_mine.reshape(features, -1)
    count = x_mine.shape[1]
    x_other = swap(x_mine, "c")

    def forward(tokens_half):
        gate = dot(gate_weight, tokens_half, 0, 0)
        upper = dot(up_weight, tokens_half, 0, 0)
        sigma = jax.nn.sigmoid(gate)
        silu = gate * sigma
        slope = upper * sigma * (1.0 + gate * (1.0 - sigma))
        return [t.astype(BF) for t in (silu * upper, silu, slope)]

    held_mine, held_other = forward(x_mine), forward(x_other)
    hidden, silu, slope = (jnp.concatenate(t, axis=1) for t in zip(held_mine, held_other))

    def pair(k):
        other = swap(row_major(dot(down[k], held_other[0], 0, 0).astype(BF)), "c")
        return row_major(dot(down[k], held_mine[0], 0, 0)) + other.astype(F32)

    arrived = [shift(pair(k).astype(BF), "y", k) for k in (2, 1, 3)]
    total = pair(0)
    for piece in arrived:
        total = total + piece.astype(F32)
    held_p = swap(jnp.stack([hidden, silu, slope]), "dp")
    teach = pair_block(teacher, c).astype(F32)
    total, held_p, teach = barrier(total.astype(BF), held_p, teach)
    sums = lax.all_to_all(total.reshape(groups, rows, count), ZX, 0, 0)
    summed = jnp.sum(sums.astype(F32), axis=0)
    errors = ((summed - teach) * factor).astype(BF)

    xs = lax.dynamic_slice_in_dim(x_mine, (1 - d) * half, half, 0)
    errors, xs, x_mine, x_other = barrier(errors, xs, x_mine, x_other)
    xp_mine = swap(xs, "dp")
    e_part = gather_zx(errors)
    xo = [lax.dynamic_slice_in_dim(t, d * half, half, 0) for t in (x_mine, x_other)]
    e_part, summed, *xo = barrier(e_part, summed.astype(BF), *xo)
    student = unpair_block(summed, c)
    keep, give = d * (groups // 2), (1 - d) * (groups // 2)
    e_got = swap(lax.dynamic_slice_in_dim(e_part, give, groups // 2, 0), "dp")
    e_pieces = {0: e_part, **{k: shift(e_part, "y", k) for k in (2, 1, 3)}}
    back = 0.0
    kept = {}
    for k in (0, 1, 3, 2):
        piece = e_pieces[k].reshape(groups * rows, count)
        if k == 1:
            piece, back = barrier(piece, back)
        other = swap(piece, "c")
        if k:
            other, back = barrier(other, back)
        piece = jnp.concatenate([piece, other], axis=1)
        kept[k] = lax.dynamic_slice_in_dim(piece.reshape(groups, rows, 2 * count), keep, groups // 2, 0)
        back = back + dot(down[(ny - k) % ny], piece, 1, 0)
    back_p = swap(back.astype(BF), "dp").astype(F32)
    up_own, gate_own, e_got = barrier((back * silu).astype(BF), (back * slope).astype(BF), e_got)
    got_pieces = {0: e_got, **{k: shift(e_got, "y", k) for k in (2, 1, 3)}}
    hidden_p, silu_p, slope_p = held_p[0], held_p[1].astype(F32), held_p[2].astype(F32)
    up_back = jnp.concatenate([up_own, (back_p * silu_p).astype(BF)], axis=1)
    gate_back = jnp.concatenate([gate_own, (back_p * slope_p).astype(BF)], axis=1)

    def assembled(pieces):
        whole = jnp.broadcast_to(pieces[0][:, None], (groups // 2, ny) + pieces[0].shape[1:])
        for k in (1, 3, 2):
            whole = lax.dynamic_update_slice_in_dim(whole, pieces[k][:, None], lax.rem(y - k + ny, ny), 1)
        return whole.reshape(half, -1)

    x_both = jnp.concatenate([*xo, xp_mine, swap(xp_mine, "c")], axis=1)
    grad_gate = dot(x_both, gate_back, 1, 1)
    grad_up = dot(x_both, up_back, 1, 1)
    grad_gate, *got_late = barrier(grad_gate, *(got_pieces[k] for k in (1, 2, 3)))
    eo, ep_mine = assembled(kept), assembled(dict(enumerate([got_pieces[0], *got_late])))
    errors_both = jnp.concatenate([eo, ep_mine, swap(ep_mine, "c")], axis=1)
    grad_down = dot(jnp.concatenate([hidden, hidden_p], axis=1), errors_both, 1, 1)
    return student, grad_gate.astype(BF), grad_up.astype(BF), grad_down.astype(BF)


def solution(mesh):
    mp = ("z", "xh", "y", "c")
    fine = Mesh(mesh.devices.reshape(2, 8, 2, 4, 2), ("dp",) + mp)
    return jax.shard_map(
        shards,
        mesh=fine,
        in_specs=(P("dp", mp), P("dp", mp), P(None, mp), P(None, mp), P(mp, None)),
        out_specs=(P("dp", mp), P("dp", mp), P("dp", mp), P(mp, "dp")),
        check_vma=False,
    )
```

```python
import functools
import math

import jax
import jax.numpy as jnp
from jax import lax
from jax.experimental import pallas as pl
from jax.experimental.pallas import tpu as pltpu
from jax.experimental.layout import Layout, with_layout_constraint
from jax.sharding import Mesh, PartitionSpec as P

BF = jnp.bfloat16
F32 = jnp.float32
ZX = ("z", "xh")


def swap(x, axis):
    return lax.ppermute(x, axis, [(0, 1), (1, 0)])


def shift(x, axis, k):
    n = lax.axis_size(axis)
    return lax.ppermute(x, axis, [(i, (i + k) % n) for i in range(n)])


def pair_block(x, c):
    xt = x.T
    half = xt.shape[1] // 2
    first, second = xt[:, :half], xt[:, half:]
    mine = jnp.where(c == 0, first, second)
    theirs = swap(jnp.where(c == 0, second, first), "c")
    low = jnp.where(c == 0, mine, theirs)
    high = jnp.where(c == 0, theirs, mine)
    return jnp.concatenate([low, high], axis=0)


def unpair_block(block, c):
    rows = block.shape[0] // 2
    low, high = block[:rows], block[rows:]
    mine = jnp.where(c == 0, low, high)
    theirs = swap(jnp.where(c == 0, high, low), "c")
    first = jnp.where(c == 0, mine, theirs)
    second = jnp.where(c == 0, theirs, mine)
    return jnp.concatenate([first, second], axis=1).T


def gather_zx(block):
    groups = lax.axis_size("z") * lax.axis_size("xh")
    copies = jnp.broadcast_to(block[None], (groups,) + block.shape)
    return lax.all_to_all(copies, ZX, 0, 0)


def gather_y(part, y, axis, *meanwhile):
    ny = lax.axis_size("y")
    part = jnp.expand_dims(part, axis)
    pieces = {k: shift(part, "y", k) for k in (2, 1, 3)}
    whole = jnp.broadcast_to(part, part.shape[:axis] + (ny,) + part.shape[axis + 1 :])
    pieces[1], whole, *meanwhile = barrier(pieces[1], whole, *meanwhile)
    for k in (1, 3, 2):
        whole = lax.dynamic_update_slice_in_dim(whole, pieces[k], lax.rem(y - k + ny, ny), axis)
    return (whole, *meanwhile)


def dot(a, b, i, j):
    return lax.dot_general(a, b, (((i,), (j,)), ((), ())), preferred_element_type=F32)


def row_major(x):
    return with_layout_constraint(x, Layout(major_to_minor=tuple(range(x.ndim))))


def barrier(*values):
    return lax.optimization_barrier(values)


def regroup_kernel(rows, y_ref, w_ref, out_ref):
    ny = out_ref.shape[0]
    groups = out_ref.shape[2] // rows
    for p in range(ny):
        k = lax.rem(p + ny - y_ref[0], ny)
        for g in range(groups):
            start = (g * ny + p) * rows
            out_ref[k, :, g * rows : (g + 1) * rows] = w_ref[:, start : start + rows]


def regroup(weight, y, ny, rows):
    units, features = weight.shape
    block = units // 3
    return pl.pallas_call(
        functools.partial(regroup_kernel, rows),
        grid_spec=pltpu.PrefetchScalarGridSpec(
            num_scalar_prefetch=1,
            grid=(units // block,),
            in_specs=[pl.BlockSpec((block, features), lambda i, y: (i, 0))],
            out_specs=pl.BlockSpec((ny, block, features // ny), lambda i, y: (0, i, 0)),
        ),
        out_shape=jax.ShapeDtypeStruct((ny, units, features // ny), weight.dtype),
        cost_estimate=pl.CostEstimate(flops=0, bytes_accessed=4 * units * features, transcendentals=0),
        name="regroup",
    )(y.reshape(1), weight)


def shards(tokens, teacher, gate_weight, up_weight, down_weight):
    c, y, d = lax.axis_index("c"), lax.axis_index("y"), lax.axis_index("dp")
    ny = lax.axis_size("y")
    features, units = gate_weight.shape
    groups = lax.axis_size("z") * lax.axis_size("xh")
    rows = features // (groups * ny)
    half = features // 2
    factor = 1.0 / math.sqrt(tokens.shape[0] * lax.axis_size("dp"))

    block, down_weight = barrier(pair_block(tokens, c), down_weight)
    part = gather_zx(block)
    down = regroup(down_weight, y, ny, rows)
    part, down = barrier(part, down)
    (x_mine,) = gather_y(part, y, 1)
    x_mine = x_mine.reshape(features, -1)
    count = x_mine.shape[1]
    x_other = swap(x_mine, "c")

    def forward(tokens_half):
        gate = dot(gate_weight, tokens_half, 0, 0)
        upper = dot(up_weight, tokens_half, 0, 0)
        sigma = jax.nn.sigmoid(gate)
        silu = gate * sigma
        slope = upper * sigma * (1.0 + gate * (1.0 - sigma))
        return [t.astype(BF) for t in (silu * upper, silu, slope)]

    held_mine, held_other = forward(x_mine), forward(x_other)
    hidden, silu, slope = (jnp.concatenate(t, axis=1) for t in zip(held_mine, held_other))

    def pair(k):
        other = swap(row_major(dot(down[k], held_other[0], 0, 0).astype(BF)), "c")
        return row_major(dot(down[k], held_mine[0], 0, 0)) + other.astype(F32)

    arrived = [shift(pair(k).astype(BF), "y", k) for k in (2, 1, 3)]
    total = pair(0)
    for piece in arrived:
        total = total + piece.astype(F32)
    held_p = swap(jnp.stack([hidden, silu, slope]), "dp")
    teach = pair_block(teacher, c).astype(F32)
    total, held_p, teach = barrier(total.astype(BF), held_p, teach)
    sums = lax.all_to_all(total.reshape(groups, rows, count), ZX, 0, 0)
    summed = jnp.sum(sums.astype(F32), axis=0)
    errors = ((summed - teach) * factor).astype(BF)

    xs = lax.dynamic_slice_in_dim(x_mine, (1 - d) * half, half, 0)
    errors, xs, x_mine, x_other = barrier(errors, xs, x_mine, x_other)
    xp_mine = swap(xs, "dp")
    e_part = gather_zx(errors)
    xo = [lax.dynamic_slice_in_dim(t, d * half, half, 0) for t in (x_mine, x_other)]
    e_part, summed, *xo = barrier(e_part, summed.astype(BF), *xo)
    student = unpair_block(summed, c)
    keep, give = d * (groups // 2), (1 - d) * (groups // 2)
    e_got = swap(lax.dynamic_slice_in_dim(e_part, give, groups // 2, 0), "dp")
    e_pieces = {0: e_part, **{k: shift(e_part, "y", k) for k in (2, 1, 3)}}
    back = 0.0
    kept = {}
    for k in (0, 1, 3, 2):
        piece = e_pieces[k].reshape(groups * rows, count)
        if k == 1:
            piece, back = barrier(piece, back)
        other = swap(piece, "c")
        if k:
            other, back = barrier(other, back)
        piece = jnp.concatenate([piece, other], axis=1)
        kept[k] = lax.dynamic_slice_in_dim(piece.reshape(groups, rows, 2 * count), keep, groups // 2, 0)
        back = back + dot(down[(ny - k) % ny], piece, 1, 0)
    back_p = swap(back.astype(BF), "dp").astype(F32)
    up_own, gate_own, e_got = barrier((back * silu).astype(BF), (back * slope).astype(BF), e_got)
    got_pieces = {0: e_got, **{k: shift(e_got, "y", k) for k in (2, 1, 3)}}
    hidden_p, silu_p, slope_p = held_p[0], held_p[1].astype(F32), held_p[2].astype(F32)
    up_back_p, gate_back_p = (back_p * silu_p).astype(BF), (back_p * slope_p).astype(BF)

    def assembled(pieces):
        whole = jnp.broadcast_to(pieces[0][:, None], (groups // 2, ny) + pieces[0].shape[1:])
        for k in (1, 3, 2):
            whole = lax.dynamic_update_slice_in_dim(whole, pieces[k][:, None], lax.rem(y - k + ny, ny), 1)
        return whole.reshape(half, -1)

    x_own = jnp.concatenate(xo, axis=1)
    xp = jnp.concatenate([xp_mine, swap(xp_mine, "c")], axis=1)
    grad_gate = dot(x_own, gate_own, 1, 1) + dot(xp, gate_back_p, 1, 1)
    grad_up = dot(x_own, up_own, 1, 1) + dot(xp, up_back_p, 1, 1)
    grad_gate, *got_late = barrier(grad_gate, *(got_pieces[k] for k in (1, 2, 3)))
    eo, ep_mine = assembled(kept), assembled(dict(enumerate([got_pieces[0], *got_late])))
    errors_both = jnp.concatenate([eo, ep_mine, swap(ep_mine, "c")], axis=1)
    grad_down = dot(jnp.concatenate([hidden, hidden_p], axis=1), errors_both, 1, 1)
    return student, grad_gate.astype(BF), grad_up.astype(BF), grad_down.astype(BF)


def solution(mesh):
    mp = ("z", "xh", "y", "c")
    fine = Mesh(mesh.devices.reshape(2, 8, 2, 4, 2), ("dp",) + mp)
    return jax.shard_map(
        shards,
        mesh=fine,
        in_specs=(P("dp", mp), P("dp", mp), P(None, mp), P(None, mp), P(mp, None)),
        out_specs=(P("dp", mp), P("dp", mp), P("dp", mp), P(mp, "dp")),
        check_vma=False,
    )
```
